32 devices in a mesh: sec: 2 (over core), grp: 4 (over z), col: 4 (over y, x).
Axes of the slice: x: 2, y: 2, z: 4, core: 2. Of those that a mesh axis runs over, the one named last changes fastest.
Arguments:
- fields: float32 [2, 64, 128, 512], P('sec', 'col', 'grp'), may hold values from -4 to 4
- soil_type: int32 [64, 128, 512], P(None, 'grp', 'col'), may hold values from 0 to 7
- surface: float32 [128, 512], P('grp', 'col'), may hold values from -8 to 8
- heat_cond: float32 [8], replicated, may hold values from 0.5 to 3
- heat_capacity: float32 [8], replicated, may hold values from 1 to 3
- porosity: float32 [8], replicated, may hold values from 0.3 to 0.55
- sat_cond: float32 [8], replicated, may hold values from 0.2 to 2
- vg_alpha: float32 [8], replicated, may hold values from 0.5 to 3
Outputs:
- advanced: float32 [2, 64, 128, 512], P('sec', 'col', 'grp')
The draws below stay inside these ranges and needn't reach their ends.
All inputs are finite; a program needn't handle non-finite values.
Results may differ from the reference program's by a relative error of at most 0.0003.
Values sent between devices are 32-bit elements; how exact they have to be, the bound alone decides.
A program may use at most 128 MiB of HBM per device.

```python
import math
import jax
import jax.numpy as jnp
from jax import lax

CX = 32
CY = 128
NZ = 64
NSOIL = 8
OUTER = 2
INNER = 3
MARGIN = 2
NX = 128
NY = 512
N_GRP = 4
N_COL = 4


def draw_fields(key, part):
    key = jax.random.fold_in(key, 11)
    temper_key, head_key = jax.random.split(key)
    temper = jnp.clip(jax.random.normal(temper_key, (NZ, NX, NY), jnp.float32), -4.0, 4.0)
    head = 1.0 + 0.6 * jnp.clip(jax.random.normal(head_key, (NZ, NX, NY), jnp.float32), -4.0, 4.0)
    return jnp.stack([temper, head])


def touch_ends(values, key, least, largest):
    place = [jax.random.randint(jax.random.fold_in(key, axis), (), 0, length) for axis, length in enumerate(values.shape)]
    main_axis = values.shape.index(max(values.shape))
    beside = place[:main_axis] + [(place[main_axis] + 1) % values.shape[main_axis]] + place[main_axis + 1:]
    return values.at[tuple(place)].set(least).at[tuple(beside)].set(largest)


def levels(rng, dims, shards, smallest, high):
    level, own = 1.0, jax.random.fold_in(rng, 6)
    for axis_at, shards_of in shards:
        draws = jnp.exp(jax.random.uniform(jax.random.fold_in(own, axis_at), (shards_of,), jnp.float32, smallest / len(shards), high / len(shards)))
        level = level * jnp.repeat(draws, dims[axis_at] // shards_of).reshape([-1 if axis == axis_at else 1 for axis in range(len(dims))])
    return level


def bell_draw(stream_key, dims, spread, limit, pieces=(), held_as=jnp.bfloat16):
    level = levels(stream_key, dims, pieces, -0.22, 0.18) if pieces else 1.0
    values = jax.random.normal(stream_key, dims, jnp.float32) * spread * level
    return jnp.minimum(jnp.maximum(values, -limit), limit).astype(held_as)


def setup_inputs(seed: int = 0) -> dict:
    streams_of = jax.random.split(jax.random.key(seed), 9)
    return {
        "fields": draw_fields(jax.random.fold_in(streams_of[8], 71), 0),
        "soil_type": touch_ends(jax.random.randint(streams_of[1], (NZ, NX, NY), 0, NSOIL), jax.random.fold_in(streams_of[1], 1), 0, NSOIL - 1).astype(jnp.int32),
        "surface": bell_draw(streams_of[2], (NX, NY), 2.0, 8.0, ((0, 4), (1, 4)), jnp.float32),
        "heat_cond": jnp.clip(jnp.exp(jax.random.uniform(streams_of[3], (NSOIL,), jnp.float32, math.log(0.5), math.log(3.0))), 0.5, 3.0),
        "heat_capacity": jnp.clip(jax.random.uniform(streams_of[4], (NSOIL,), jnp.float32, 1.0, 3.0), 1.0, 3.0),
        "porosity": jnp.clip(jax.random.uniform(streams_of[5], (NSOIL,), jnp.float32, 0.3, 0.55), 0.3, 0.55),
        "sat_cond": jnp.clip(jnp.exp(jax.random.uniform(streams_of[6], (NSOIL,), jnp.float32, math.log(0.2), math.log(2.0))), 0.2, 2.0),
        "vg_alpha": jnp.clip(jnp.exp(jax.random.uniform(streams_of[7], (NSOIL,), jnp.float32, math.log(0.5), math.log(3.0))), 0.5, 3.0),
    }


delta_freeze = 0.5
latent = 4.0
ice_cond = 1.0
heat_side = 0.2
heat_vert = 8.0
storage = 0.001
residual_share = 0.1
flow_side = 0.002
flow_vert = 1.5
impedance = 2.0
drainage = 1.0
elevation = 0.1

def lookup(soil_wide, soil_table):
    summed = jnp.zeros(soil_wide.shape, jnp.float32)
    for soil_kind in range(soil_table.shape[0]):
        summed = summed + jnp.where(soil_wide == soil_kind, soil_table[soil_kind], jnp.float32(0.0))
    return summed

def tridiagonal(sub_diag, main_diag, super_diag, right_side):

    def forward(carried, level_row):
        ratio_above, value_above = carried
        sub_level, main_level, super_level, right_level = level_row
        divisor = main_level - sub_level * ratio_above
        ratio_new = super_level / divisor
        value_new = (right_level - sub_level * value_above) / divisor
        return ((ratio_new, value_new), (ratio_new, value_new))
    plane_zero = jnp.zeros(main_diag.shape[1:], main_diag.dtype)
    unused_end, (ratios, values) = lax.scan(forward, (plane_zero, plane_zero), (sub_diag, main_diag, super_diag, right_side))

    def backward(below_value, level_row):
        ratio_level, value_level = level_row
        solved_level = value_level - ratio_level * below_value
        return (solved_level, solved_level)
    unused_top, solved = lax.scan(backward, plane_zero, (ratios, values), reverse=True)
    return solved

def harmonic(first_coef, second_coef):
    return 2.0 * first_coef * second_coef / (first_coef + second_coef)

def pad_levels(vertical, before, after):
    return jnp.pad(vertical, ((before, after), (0, 0), (0, 0)))

def soil_state(temper_wide, pressure_wide, soil_wide, tables):
    liquid = jax.nn.sigmoid(temper_wide / delta_freeze)
    alpha_cell = lookup(soil_wide, tables[4])
    poro_cell = lookup(soil_wide, tables[2])
    suction = jnp.maximum(-pressure_wide, 0.0)
    saturation = 1.0 / jnp.sqrt(1.0 + (alpha_cell * suction) ** 2)
    moisture = poro_cell * (residual_share + (1.0 - residual_share) * saturation)
    return (liquid, alpha_cell, poro_cell, suction, saturation, moisture)

def heat_setup(temper_wide, pressure_wide, soil_wide, surface, tables):
    state = soil_state(temper_wide, pressure_wide, soil_wide, tables)
    liquid, moisture = (state[0], state[5])
    conductivity = lookup(soil_wide, tables[0]) * (1.0 + ice_cond * moisture * (1.0 - liquid))
    centre = conductivity[:, 1:-1, 1:-1]
    east_coef = heat_side * harmonic(centre, conductivity[:, 2:, 1:-1])
    west_coef = heat_side * harmonic(centre, conductivity[:, :-2, 1:-1])
    north_coef = heat_side * harmonic(centre, conductivity[:, 1:-1, 2:])
    south_coef = heat_side * harmonic(centre, conductivity[:, 1:-1, :-2])
    vertical = heat_vert * harmonic(centre[:-1], centre[1:])
    top_cond = 2.0 * heat_vert * centre[0]
    sub_diag = -pad_levels(vertical, 1, 0)
    super_diag = -pad_levels(vertical, 0, 1)
    main_static = pad_levels(vertical, 1, 0) + pad_levels(vertical, 0, 1)
    main_static = main_static.at[0].add(top_cond)
    capacity = lookup(soil_wide[:, 1:-1, 1:-1], tables[1])
    latent_moist = latent * moisture[:, 1:-1, 1:-1]
    fixed_source = capacity * temper_wide[:, 1:-1, 1:-1] + latent_moist * liquid[:, 1:-1, 1:-1]
    fixed_source = fixed_source.at[0].add(top_cond * surface)
    return (sub_diag, super_diag, main_static, capacity, latent_moist, fixed_source, east_coef, west_coef, north_coef, south_coef)

def heat_iterate(current_wide, heat_pack):
    sub_diag, super_diag, main_static, capacity, latent_moist, fixed_source, east_coef, west_coef, north_coef, south_coef = heat_pack
    current = current_wide[:, 1:-1, 1:-1]
    fraction = jax.nn.sigmoid(current / delta_freeze)
    apparent = capacity + latent_moist * fraction * (1.0 - fraction) / delta_freeze
    enthalpy = capacity * current + latent_moist * fraction
    lateral = east_coef * (current_wide[:, 2:, 1:-1] - current) + west_coef * (current_wide[:, :-2, 1:-1] - current)
    lateral = lateral + north_coef * (current_wide[:, 1:-1, 2:] - current) + south_coef * (current_wide[:, 1:-1, :-2] - current)
    right_side = apparent * current - enthalpy + fixed_source + lateral
    return tridiagonal(sub_diag, apparent + main_static, super_diag, right_side)

def flow_setup(temper_wide, pressure_wide, soil_wide, tables):
    liquid, alpha_cell, poro_cell, suction, saturation, moisture = soil_state(temper_wide, pressure_wide, soil_wide, tables)
    hydraulic = lookup(soil_wide, tables[3]) * saturation ** 3 * jnp.exp(-impedance * (1.0 - liquid))
    capacity = storage + poro_cell * (1.0 - residual_share) * alpha_cell ** 2 * suction * saturation ** 3
    inner_cond = hydraulic[:, 1:-1, 1:-1]
    vertical = flow_vert * 0.5 * (inner_cond[:-1] + inner_cond[1:])
    side_coef = flow_side * inner_cond
    above_pad = pad_levels(vertical, 1, 0)
    below_pad = pad_levels(vertical, 0, 1)
    inner_cap = capacity[:, 1:-1, 1:-1]
    main_diag = inner_cap + above_pad + below_pad + 4.0 * side_coef
    gravity = elevation * (above_pad - below_pad)
    gravity = gravity.at[-1].add(-elevation * drainage * inner_cond[-1])
    base_source = inner_cap * pressure_wide[:, 1:-1, 1:-1] + gravity
    return (-above_pad, -below_pad, main_diag, side_coef, base_source)

def flow_sweep(iterate, flow_pack):
    sub_diag, super_diag, main_diag, side_coef, base_source = flow_pack
    for inner_index in range(INNER):
        neighbours = iterate[:, 2:, 1:-1] + iterate[:, :-2, 1:-1] + iterate[:, 1:-1, 2:] + iterate[:, 1:-1, :-2]
        solved = tridiagonal(sub_diag, main_diag, super_diag, base_source + side_coef * neighbours)
        iterate = iterate.at[:, 1:-1, 1:-1].set(solved)
    return iterate[:, MARGIN:iterate.shape[1] - MARGIN, MARGIN:iterate.shape[2] - MARGIN]

def widen_grid(field_in, margin_width):
    return jnp.pad(field_in, ((0, 0), (margin_width, margin_width), (margin_width, margin_width)))

def reference(fields, soil_type, surface, heat_cond, heat_capacity, porosity, sat_cond, vg_alpha):
    tables = (heat_cond, heat_capacity, porosity, sat_cond, vg_alpha)
    temper = fields[0]
    pressure = fields[1]
    heat_pack = heat_setup(widen_grid(temper, 1), widen_grid(pressure, 1), widen_grid(soil_type, 1), surface, tables)
    current = temper
    for outer_index in range(OUTER):
        current = heat_iterate(widen_grid(current, 1), heat_pack)
    flow_pack = flow_setup(widen_grid(temper, MARGIN), widen_grid(pressure, MARGIN), widen_grid(soil_type, MARGIN), tables)
    tile_ids = jnp.arange(N_GRP * N_COL, dtype=jnp.int32)
    anchor = jnp.zeros((), jnp.int32)
    pressure_now = pressure
    for outer_index in range(OUTER):
        padded = widen_grid(pressure_now, MARGIN)

        def one_tile(tile_id):
            start_row = (tile_id // N_COL * CX).astype(jnp.int32)
            start_col = (tile_id % N_COL * CY).astype(jnp.int32)
            tile_block = lax.dynamic_slice(padded, (anchor, start_row, start_col), (NZ, CX + 2 * MARGIN, CY + 2 * MARGIN))
            tile_pack = tuple((lax.dynamic_slice(coef_field, (anchor, start_row, start_col), (NZ, CX + 2 * MARGIN - 2, CY + 2 * MARGIN - 2)) for coef_field in flow_pack))
            return flow_sweep(tile_block, tile_pack)
        result = lax.map(one_tile, tile_ids)
        pressure_now = result.reshape(N_GRP, N_COL, NZ, CX, CY).transpose(2, 0, 3, 1, 4).reshape(NZ, N_GRP * CX, N_COL * CY)
    return jnp.stack([current, pressure_now])
```

```python
import functools
import jax
import jax.numpy as jnp
from jax import lax
from jax.experimental import pallas as pl
from jax.experimental.pallas import tpu as pltpu
from jax.sharding import PartitionSpec as P

OUTER = 2
INNER = 3
CHUNK = 4
ROWS = 40
COLS = 256
MESH = pl.DeviceIdType.MESH

heat_side = 0.2
heat_vert = 8.0
storage = 0.001
flow_side = 0.002
flow_vert = 1.5
elevation = 0.1


def harmonic(a, b):
    return 2.0 * a * b / (a + b)


def sigmoid2(x):
    return 1.0 / (1.0 + jnp.exp(-2.0 * x))


def kernel(
    n_grp, n_col, fields, soil, surface, tab, out,
    own_m, oth_m, own_r, own_rc, oth_rc, own_cs, own_c, oth_c,
    soil_r, soil_rc, soil_cs, soil_c,
    res, it_r, it_rc, it_cs, it_c, res2,
    xw, vb, bI, sI, aI, rI, kb,
    loc_sem, a2a_s, a2a_r, sec_s, sec_r, row_s, row_r, col_s, col_r, fin_s, fin_r,
):
    sec = lax.axis_index("sec")
    g = lax.axis_index("grp")
    c = lax.axis_index("col")
    nz, nx, ny = soil.shape
    zs = fields.shape[1]
    is_heat = sec == 0
    up_ok, down_ok = g > 0, g < n_grp - 1
    left_ok, right_ok = c > 0, c < n_col - 1

    barrier = pltpu.get_barrier_semaphore()
    for k in range(1, n_col):
        pl.semaphore_signal(barrier, inc=1, device_id={"col": lax.rem(c + k, n_col)}, device_id_type=MESH)
    pl.semaphore_signal(barrier, inc=1, device_id={"sec": 1 - sec}, device_id_type=MESH)

    @pl.when(up_ok)
    def _():
        pl.semaphore_signal(barrier, inc=1, device_id={"grp": g - 1}, device_id_type=MESH)

    @pl.when(down_ok)
    def _():
        pl.semaphore_signal(barrier, inc=1, device_id={"grp": g + 1}, device_id_type=MESH)

    beside = jnp.where(up_ok, 1, 0) + jnp.where(down_ok, 1, 0)
    pl.semaphore_wait(barrier, n_col + beside)

    def remote(src, dst, s, r, **where):
        return pltpu.make_async_remote_copy(
            src_ref=src, dst_ref=dst, send_sem=s, recv_sem=r, device_id=where, device_id_type=MESH
        )

    def two_way(axis, index, count, sends, dst, ssem, rsem, low_ok, high_ok):
        ahead = remote(sends[0], dst.at[0], ssem.at[0], rsem.at[0], **{axis: lax.rem(index + 1, count)})
        back = remote(sends[1], dst.at[1], ssem.at[1], rsem.at[1], **{axis: lax.rem(index + count - 1, count)})

        def start():
            @pl.when(high_ok)
            def _():
                ahead.start()

            @pl.when(low_ok)
            def _():
                back.start()

        def wait():
            @pl.when(high_ok)
            def _():
                ahead.wait_send()
                back.wait_recv()

            @pl.when(low_ok)
            def _():
                back.wait_send()
                ahead.wait_recv()

            @pl.when(jnp.logical_not(low_ok))
            def _():
                dst[0] = jnp.zeros(dst.shape[1:], dst.dtype)

            @pl.when(jnp.logical_not(high_ok))
            def _():
                dst[1] = jnp.zeros(dst.shape[1:], dst.dtype)

        return start, wait

    def rows_of(src, dst, slot):
        sends = (src.at[:, pl.ds(nx - 8, 8), :], src.at[:, pl.ds(0, 8), :])
        return two_way("grp", g, n_grp, sends, dst, row_s.at[slot], row_r.at[slot], up_ok, down_ok)

    def cols_of(src, dst, slot):
        return two_way(
            "col", c, n_col, (src.at[0], src.at[1]), dst, col_s.at[slot], col_r.at[slot], left_ok, right_ok
        )

    lane = lax.broadcasted_iota(jnp.int32, (ROWS, ny), 1)
    sub8 = lax.broadcasted_iota(jnp.int32, (8, ny), 0)

    def levels(body, carry, down=True):
        def chunk(i, carry):
            for u in range(CHUNK):
                step = i * CHUNK + u
                carry = body(step if down else nz - 1 - step, carry)
            return carry

        return lax.fori_loop(0, nz // CHUNK, chunk, carry)

    def pack(m, r2, rc, cs):
        def body(z, carry):
            ahead, back = carry
            tile = jnp.where(sub8 < 4, r2[1, z], r2[0, z])
            rc[z] = tile
            plane = jnp.concatenate([m[z], tile], axis=0)
            mine = lax.shift_right_logical(lane, 1) == z
            ahead = jnp.where(mine, pltpu.roll(plane, lax.rem(2 * z + 2, ny), 1), ahead)
            back = jnp.where(mine, pltpu.roll(plane, 2 * z, 1), back)
            return (ahead, back)

        zero = jnp.zeros((ROWS, ny), m.dtype)
        ahead, back = levels(body, (zero, zero))
        cs[0] = ahead
        cs[1] = back

    def wide(m, rc, cc, z):
        tile = jnp.concatenate([m[z], rc[z]], axis=0)
        right = pltpu.roll(cc[1], lax.rem(ny - 2 * z, ny), 1)
        left = pltpu.roll(cc[0], ny - 2 - 2 * z, 1)
        return jnp.concatenate([tile, jnp.where(lane < 64, right, left)], axis=1)

    soil_start, soil_wait = rows_of(soil, soil_r, 0)
    local = pltpu.make_async_copy(
        fields.at[0, :, :, pl.ds(pl.multiple_of(c * ny, ny), ny)], own_m.at[pl.ds(c * zs, zs)], loc_sem.at[0]
    )
    moves = []
    for k in range(1, n_col):
        to = lax.rem(c + k, n_col)
        moves.append(
            remote(
                fields.at[0, :, :, pl.ds(pl.multiple_of(to * ny, ny), ny)],
                own_m.at[pl.ds(c * zs, zs)],
                a2a_s.at[k - 1], a2a_r.at[k - 1], col=to,
            )
        )
    for move in moves:
        move.start()
    local.start()
    soil_start()
    soil_wait()
    pack(soil, soil_r, soil_rc, soil_cs)
    soilc_start, soilc_wait = cols_of(soil_cs, soil_c, 0)
    soilc_start()
    local.wait()
    for move in moves:
        move.wait()

    other = 1 - sec
    swap_m = remote(own_m, oth_m, sec_s.at[0], sec_r.at[0], sec=other)
    swap_r = remote(own_rc, oth_rc, sec_s.at[1], sec_r.at[1], sec=other)
    swap_c = remote(own_c, oth_c, sec_s.at[2], sec_r.at[2], sec=other)
    row_start, row_wait = rows_of(own_m, own_r, 1)
    row_start()
    swap_m.start()
    row_wait()
    pack(own_m, own_r, own_rc, own_cs)
    col_start, col_wait = cols_of(own_cs, own_c, 1)
    col_start()
    swap_r.start()
    col_wait()
    swap_c.start()
    soilc_wait()
    swap_m.wait()
    swap_r.wait()
    swap_c.wait()

    own = (own_m, own_rc, own_c)
    oth = (oth_m, oth_rc, oth_c)

    def looker(kind):
        b0, b1, b2 = (kind & 1) != 0, (kind & 2) != 0, (kind & 4) != 0

        def look(row):
            t = [tab[row, i] for i in range(8)]
            q = [jnp.where(b0, t[2 * i + 1], t[2 * i]) for i in range(4)]
            return jnp.where(b2, jnp.where(b1, q[3], q[2]), jnp.where(b1, q[1], q[0]))

        return look

    def state(temper, head, look):
        liquid = sigmoid2(temper)
        alpha, poro = look(4), look(2)
        suction = jnp.maximum(-head, 0.0)
        a_s = alpha * suction
        satur = lax.rsqrt(1.0 + a_s * a_s)
        return liquid, alpha, poro, suction, satur

    one = jnp.ones((ROWS, COLS), jnp.float32)
    row_i = lax.broadcasted_iota(jnp.int32, (ROWS, COLS), 0)
    col_i = lax.broadcasted_iota(jnp.int32, (ROWS, COLS), 1)
    free = ((row_i <= nx) | (row_i == ROWS - 1)) & ((col_i <= ny) | (col_i == COLS - 1))

    def heat_setup():
        kb[0] = one
        kb[nz + 1] = one

        def first(z, carry):
            temper, head, kind = wide(*own, z), wide(*oth, z), wide(soil, soil_rc, soil_c, z)
            look = looker(kind)
            liquid, alpha, poro, suction, satur = state(temper, head, look)
            moist = poro * (0.1 + 0.9 * satur)
            kb[z + 1] = look(0) * (1.0 + moist * (1.0 - liquid))
            xw[z] = temper
            cap = looker(soil[z])(1)
            lm = 4.0 * moist[:nx, :ny]
            bI[z, :nx, :ny] = cap
            bI[z, :nx, ny:] = lm
            sI[z, :nx, :ny] = cap * temper[:nx, :ny] + lm * liquid[:nx, :ny]
            return carry

        levels(first, 0)

        def second(z, carry):
            kap = kb[z + 1]
            mid = kap[:nx, :ny]
            sI[z, :nx, ny:] = heat_side * harmonic(mid, pltpu.roll(kap, ROWS - 1, 0)[:nx, :ny])
            aI[z, :nx, :ny] = heat_side * harmonic(mid, pltpu.roll(kap, 1, 0)[:nx, :ny])
            aI[z, :nx, ny:] = heat_side * harmonic(mid, pltpu.roll(kap, COLS - 1, 1)[:nx, :ny])
            rI[z, :nx, :ny] = heat_side * harmonic(mid, pltpu.roll(kap, 1, 1)[:nx, :ny])
            has = jnp.where(z < nz - 1, heat_vert, 0.0)
            rI[z, :nx, ny:] = has * harmonic(mid, kb[z + 2, :nx, :ny])
            return carry

        levels(second, 0)
        sI[0, :nx, :ny] = sI[0, :nx, :ny] + 2.0 * heat_vert * kb[1, :nx, :ny] * surface[...]

    def heat_solve(dst):
        def forward(z, carry):
            above, ratio, value = carry
            x = xw[z]
            t = x[:nx, :ny]
            cap, lm = bI[z, :nx, :ny], bI[z, :nx, ny:]
            f = sigmoid2(t)
            apparent = cap + lm * f * (1.0 - f) * 2.0
            lateral = sI[z, :nx, ny:] * (pltpu.roll(x, ROWS - 1, 0)[:nx, :ny] - t)
            lateral += aI[z, :nx, :ny] * (pltpu.roll(x, 1, 0)[:nx, :ny] - t)
            lateral += aI[z, :nx, ny:] * (pltpu.roll(x, COLS - 1, 1)[:nx, :ny] - t)
            lateral += rI[z, :nx, :ny] * (pltpu.roll(x, 1, 1)[:nx, :ny] - t)
            right = apparent * t - (cap * t + lm * f) + sI[z, :nx, :ny] + lateral
            below = rI[z, :nx, ny:]
            inv = 1.0 / (apparent + above + below + above * ratio)
            ratio = -below * inv
            value = (right + above * value) * inv
            vb[z, :nx, :ny] = value
            vb[z, :nx, ny:] = ratio
            return (below, ratio, value)

        zero = jnp.zeros((nx, ny), jnp.float32)
        levels(forward, (2.0 * heat_vert * kb[1, :nx, :ny], zero, zero))

        def backward(z, lower):
            solved = vb[z, :nx, :ny] - vb[z, :nx, ny:] * lower
            dst[z] = solved
            return solved

        levels(backward, zero, down=False)

    def flow_setup():
        kb[0] = one
        kb[nz + 1] = one

        def first(z, carry):
            temper, head, kind = wide(*oth, z), wide(*own, z), wide(soil, soil_rc, soil_c, z)
            look = looker(kind)
            liquid, alpha, poro, suction, satur = state(temper, head, look)
            cube = satur * satur * satur
            kb[z + 1] = look(3) * cube * jnp.exp(-2.0 * (1.0 - liquid))
            vb[z] = storage + poro * 0.9 * alpha * alpha * suction * cube
            xw[z] = head
            return carry

        levels(first, 0)

        def second(z, carry):
            above, ratio = carry
            hyd, cap, x = kb[z + 1], vb[z], xw[z]
            has = jnp.where(z < nz - 1, flow_vert * 0.5, 0.0)
            drain = jnp.where(z < nz - 1, 0.0, elevation)
            below = has * (hyd + kb[z + 2])
            side = flow_side * hyd
            inv = 1.0 / (cap + above + below + 4.0 * side - above * ratio)
            ratio = below * inv
            base = cap * x + elevation * (above - below) - drain * hyd
            bI[z] = jnp.where(free, base * inv, x)
            sI[z] = jnp.where(free, side * inv, 0.0)
            aI[z] = jnp.where(free, above * inv, 0.0)
            rI[z] = jnp.where(free, ratio, 0.0)
            return (below, ratio)

        zero = jnp.zeros((ROWS, COLS), jnp.float32)
        levels(second, (zero, zero))

    def flow_solve(dst):
        for inner in range(INNER):
            last = inner == INNER - 1
            h, w = (nx, ny) if last else (ROWS, COLS)

            def forward(z, value):
                x = xw[z]
                near = pltpu.roll(x, 1, 0) + pltpu.roll(x, ROWS - 1, 0)
                near = near[:h, :w] + (pltpu.roll(x, 1, 1) + pltpu.roll(x, COLS - 1, 1))[:h, :w]
                value = bI[z, :h, :w] + sI[z, :h, :w] * near + aI[z, :h, :w] * value
                vb[z, :h, :w] = value
                return value

            zero = jnp.zeros((h, w), jnp.float32)
            levels(forward, zero)

            def backward(z, lower):
                solved = vb[z, :h, :w] + rI[z, :h, :w] * lower
                if last:
                    dst[z] = solved
                else:
                    xw[z] = solved
                return solved

            levels(backward, zero, down=False)

    @pl.when(is_heat)
    def _():
        heat_setup()
        heat_solve(res)

    @pl.when(jnp.logical_not(is_heat))
    def _():
        flow_setup()
        flow_solve(res)

    itr_start, itr_wait = rows_of(res, it_r, 2)
    itr_start()
    itr_wait()
    pack(res, it_r, it_rc, it_cs)
    itc_start, itc_wait = cols_of(it_cs, it_c, 2)
    itc_start()
    itc_wait()

    @pl.when(is_heat)
    def _():
        def fill(z, carry):
            xw[z] = wide(res, it_rc, it_c, z)
            return carry

        levels(fill, 0)
        heat_solve(res2)

    @pl.when(jnp.logical_not(is_heat))
    def _():
        def fill(z, carry):
            x = wide(res, it_rc, it_c, z)
            xw[z] = x
            bI[z] = jnp.where(free, bI[z], x)
            return carry

        levels(fill, 0)
        flow_solve(res2)

    lanes = pl.ds(pl.multiple_of(c * ny, ny), ny)
    moves = []
    for k in range(1, n_col):
        to = lax.rem(c + k, n_col)
        moves.append(
            remote(res2.at[pl.ds(to * zs, zs)], out.at[0, :, :, lanes], fin_s.at[k - 1], fin_r.at[k - 1], col=to)
        )
    local = pltpu.make_async_copy(res2.at[pl.ds(c * zs, zs)], out.at[0, :, :, lanes], loc_sem.at[1])
    for move in moves:
        move.start()
    local.start()
    local.wait()
    for move in moves:
        move.wait()


def solution(mesh):
    n_grp, n_col = mesh.shape["grp"], mesh.shape["col"]

    def on_device(fields, soil_type, surface, heat_cond, heat_capacity, porosity, sat_cond, vg_alpha):
        tab = jnp.stack([heat_cond, heat_capacity, porosity, sat_cond, vg_alpha])
        nz, nx, ny = soil_type.shape
        f32, i32 = jnp.float32, jnp.int32
        whole = lambda t: pltpu.VMEM((nz, nx, ny), t)
        tile = lambda t: pltpu.VMEM((nz, 8, ny), t)
        pair = lambda t: pltpu.VMEM((2, nz, 8, ny), t)
        strip = lambda t: pltpu.VMEM((2, ROWS, ny), t)
        field = pltpu.VMEM((nz, ROWS, COLS), f32)
        dma = lambda *s: pltpu.SemaphoreType.DMA(s)
        scratch = [
            whole(f32), whole(f32), pair(f32), tile(f32), tile(f32), strip(f32), strip(f32), strip(f32),
            pair(i32), tile(i32), strip(i32), strip(i32),
            whole(f32), pair(f32), tile(f32), strip(f32), strip(f32), whole(f32),
            field, field, field, field, field, field, pltpu.VMEM((nz + 2, ROWS, COLS), f32),
            dma(2), dma(n_col - 1), dma(n_col - 1), dma(3), dma(3), dma(3, 2), dma(3, 2), dma(3, 2), dma(3, 2),
            dma(n_col - 1), dma(n_col - 1),
        ]
        anywhere = pl.BlockSpec(memory_space=pl.ANY)
        vmem = pl.BlockSpec(memory_space=pltpu.VMEM)
        return pl.pallas_call(
            functools.partial(kernel, n_grp, n_col),
            out_shape=jax.ShapeDtypeStruct(fields.shape, f32),
            in_specs=[anywhere, vmem, vmem, pl.BlockSpec(memory_space=pltpu.SMEM)],
            out_specs=anywhere,
            scratch_shapes=scratch,
            compiler_params=pltpu.CompilerParams(
                collective_id=0, has_side_effects=True, vmem_limit_bytes=48 * 2**20
            ),
            name="step",
        )(fields, soil_type, surface, tab)

    in_specs = (
        P("sec", "col", "grp", None), P(None, "grp", "col"), P("grp", "col"),
        P(), P(), P(), P(), P(),
    )
    return jax.shard_map(
        on_device, mesh=mesh, in_specs=in_specs, out_specs=P("sec", "col", "grp", None), check_vma=False
    )
```

```python
import functools
import jax
import jax.numpy as jnp
from jax import lax
from jax.experimental import pallas as pl
from jax.experimental.pallas import tpu as pltpu
from jax.sharding import PartitionSpec as P

OUTER = 2
INNER = 3
CHUNK = 4
ROWS = 40
COLS = 256
MESH = pl.DeviceIdType.MESH

heat_side = 0.2
heat_vert = 8.0
storage = 0.001
flow_side = 0.002
flow_vert = 1.5
elevation = 0.1


def harmonic(a, b):
    return 2.0 * a * b / (a + b)


def sigmoid2(x):
    return 1.0 / (1.0 + jnp.exp(-2.0 * x))


def kernel(
    n_grp, n_col, fields, soil_in, surface_in, tab_0, tab_1, tab_2, tab_3, tab_4, out,
    soil, surface, tab,
    own_m, oth_m, own_rc, oth_rc, own_cs, own_c, oth_c,
    soil_rc, soil_cs, soil_c,
    res, it_rc, it_cs, it_c, res2,
    xw, vb, bI, sI, aI, rI, kb,
    loc_sem, a2a_s, a2a_r, sec_s, sec_r, edge_s, edge_r, fin_s, fin_r,
):
    sec = lax.axis_index("sec")
    g = lax.axis_index("grp")
    c = lax.axis_index("col")
    nz, nx, ny = soil.shape
    zs = fields.shape[1]
    is_heat = sec == 0

    def inside(dg, dc):
        ok = None
        for at, d, count in ((g, dg, n_grp), (c, dc, n_col)):
            if d:
                here = at < count - 1 if d > 0 else at > 0
                ok = here if ok is None else jnp.logical_and(ok, here)
        return ok

    way = [(1, 0), (-1, 0), (0, 1), (0, -1), (1, 1), (-1, 1), (1, -1), (-1, -1)]

    def at_way(dg, dc):
        return {"grp": lax.rem(g + dg + n_grp, n_grp), "col": lax.rem(c + dc + n_col, n_col)}

    barrier = pltpu.get_barrier_semaphore()
    for buffer in (own_rc, soil_rc, it_rc, own_c, soil_c, it_c):
        buffer[...] = jnp.zeros(buffer.shape, buffer.dtype)
    met = n_col
    for k in range(1, n_col):
        pl.semaphore_signal(barrier, inc=1, device_id={"col": lax.rem(c + k, n_col)}, device_id_type=MESH)
    pl.semaphore_signal(barrier, inc=1, device_id={"sec": 1 - sec}, device_id_type=MESH)
    for dg, dc in way:
        if dg:
            met = met + jnp.where(inside(dg, dc), 1, 0)

            @pl.when(inside(dg, dc))
            def _():
                pl.semaphore_signal(barrier, inc=1, device_id=at_way(dg, dc), device_id_type=MESH)

    pl.semaphore_wait(barrier, met)

    def remote(src, dst, s, r, **where):
        return pltpu.make_async_remote_copy(
            src_ref=src, dst_ref=dst, send_sem=s, recv_sem=r, device_id=where, device_id_type=MESH
        )

    def edges(m, rc, cs, cc, slot):
        low, high = pl.ds(0, 2), pl.ds(nx - 2, 2)
        above, below = pl.ds(ROWS - 2, 2), pl.ds(nx, 2)
        parts = [
            (m.at[:, high, :], rc.at[:, pl.ds(6, 2), :]),
            (m.at[:, low, :], rc.at[:, pl.ds(0, 2), :]),
            (cs.at[0], cc.at[0, pl.ds(0, nx), :]),
            (cs.at[1], cc.at[1, pl.ds(0, nx), :]),
            (cs.at[0, high, :], cc.at[0, above, :]),
            (cs.at[0, low, :], cc.at[0, below, :]),
            (cs.at[1, high, :], cc.at[1, above, :]),
            (cs.at[1, low, :], cc.at[1, below, :]),
        ]
        copies = [
            remote(src, dst, edge_s.at[slot, i], edge_r.at[slot, i], **at_way(*way[i]))
            for i, (src, dst) in enumerate(parts)
        ]

        def start(these):
            for i in these:
                @pl.when(inside(*way[i]))
                def _():
                    copies[i].start()

        start((0, 1))
        pack(m, cs)
        start(range(2, 8))

        def wait():
            for i, (dg, dc) in enumerate(way):
                @pl.when(inside(dg, dc))
                def _():
                    copies[i].wait_send()

                @pl.when(inside(-dg, -dc))
                def _():
                    copies[i].wait_recv()

        return wait

    lane = lax.broadcasted_iota(jnp.int32, (ROWS, ny), 1)

    def levels(body, carry, down=True):
        def chunk(i, carry):
            for u in range(CHUNK):
                step = i * CHUNK + u
                carry = body(step if down else nz - 1 - step, carry)
            return carry

        return lax.fori_loop(0, nz // CHUNK, chunk, carry)

    def pack(m, cs):
        pair = lax.shift_right_logical(lax.broadcasted_iota(jnp.int32, (nx, ny), 1), 1)

        def body(z, carry):
            ahead, back = carry
            plane = m[z]
            ahead = jnp.where(pair == z, pltpu.roll(plane, lax.rem(2 * z + 2, ny), 1), ahead)
            back = jnp.where(pair == z, pltpu.roll(plane, 2 * z, 1), back)
            return (ahead, back)

        zero = jnp.zeros((nx, ny), m.dtype)
        ahead, back = levels(body, (zero, zero))
        cs[0] = ahead
        cs[1] = back

    def wide(m, rc, cc, z):
        tile = jnp.concatenate([m[z], rc[z]], axis=0)
        right = pltpu.roll(cc[1], lax.rem(ny - 2 * z, ny), 1)
        left = pltpu.roll(cc[0], ny - 2 - 2 * z, 1)
        return jnp.concatenate([tile, jnp.where(lane < 64, right, left)], axis=1)

    tabs = (tab_0, tab_1, tab_2, tab_3, tab_4)
    loads = [pltpu.make_async_copy(soil_in, soil, loc_sem.at[2]), pltpu.make_async_copy(surface_in, surface, loc_sem.at[3])]
    loads += [pltpu.make_async_copy(t, tab.at[i], loc_sem.at[4 + i]) for i, t in enumerate(tabs)]
    local = pltpu.make_async_copy(
        fields.at[0, :, :, pl.ds(pl.multiple_of(c * ny, ny), ny)], own_m.at[pl.ds(c * zs, zs)], loc_sem.at[0]
    )
    moves = []
    for k in range(1, n_col):
        to = lax.rem(c + k, n_col)
        moves.append(
            remote(
                fields.at[0, :, :, pl.ds(pl.multiple_of(to * ny, ny), ny)],
                own_m.at[pl.ds(c * zs, zs)],
                a2a_s.at[k - 1], a2a_r.at[k - 1], col=to,
            )
        )
    for move in moves:
        move.start()
    local.start()
    for load in loads:
        load.start()
    loads[0].wait()
    soil_wait = edges(soil, soil_rc, soil_cs, soil_c, 0)

    other = 1 - sec
    swaps = []

    def swap(src, dst):
        i = len(swaps)
        swaps.append(remote(src, dst, sec_s.at[i], sec_r.at[i], sec=other))
        swaps[i].start()

    local.wait()
    swap(own_m.at[pl.ds(c * zs, zs)], oth_m.at[pl.ds(c * zs, zs)])
    for k, move in enumerate(moves):
        move.wait_recv()
        came = lax.rem(c + n_col - 1 - k, n_col)
        swap(own_m.at[pl.ds(came * zs, zs)], oth_m.at[pl.ds(came * zs, zs)])
    own_wait = edges(own_m, own_rc, own_cs, own_c, 1)
    own_wait()
    swap(own_rc, oth_rc)
    swap(own_c, oth_c)
    for move in moves:
        move.wait_send()
    soil_wait()
    for load in loads[1:]:
        load.wait()
    for one_swap in swaps:
        one_swap.wait()

    own = (own_m, own_rc, own_c)
    oth = (oth_m, oth_rc, oth_c)

    def looker(kind):
        b0, b1, b2 = (kind & 1) != 0, (kind & 2) != 0, (kind & 4) != 0

        def look(row):
            t = [tab[row, i] for i in range(8)]
            q = [jnp.where(b0, t[2 * i + 1], t[2 * i]) for i in range(4)]
            return jnp.where(b2, jnp.where(b1, q[3], q[2]), jnp.where(b1, q[1], q[0]))

        return look

    def state(temper, head, look):
        liquid = sigmoid2(temper)
        alpha, poro = look(4), look(2)
        suction = jnp.maximum(-head, 0.0)
        a_s = alpha * suction
        satur = lax.rsqrt(1.0 + a_s * a_s)
        return liquid, alpha, poro, suction, satur

    one = jnp.ones((ROWS, COLS), jnp.float32)
    row_i = lax.broadcasted_iota(jnp.int32, (ROWS, COLS), 0)
    col_i = lax.broadcasted_iota(jnp.int32, (ROWS, COLS), 1)
    free = ((row_i <= nx) | (row_i == ROWS - 1)) & ((col_i <= ny) | (col_i == COLS - 1))

    def heat_setup():
        kb[0] = one
        kb[nz + 1] = one

        def first(z, carry):
            temper, head, kind = wide(*own, z), wide(*oth, z), wide(soil, soil_rc, soil_c, z)
            look = looker(kind)
            liquid, alpha, poro, suction, satur = state(temper, head, look)
            moist = poro * (0.1 + 0.9 * satur)
            kb[z + 1] = look(0) * (1.0 + moist * (1.0 - liquid))
            xw[z] = temper
            cap = looker(soil[z])(1)
            lm = 4.0 * moist[:nx, :ny]
            bI[z, :nx, :ny] = cap
            bI[z, :nx, ny:] = lm
            sI[z, :nx, :ny] = cap * temper[:nx, :ny] + lm * liquid[:nx, :ny]
            return carry

        levels(first, 0)

        def second(z, carry):
            kap = kb[z + 1]
            mid = kap[:nx, :ny]
            sI[z, :nx, ny:] = heat_side * harmonic(mid, pltpu.roll(kap, ROWS - 1, 0)[:nx, :ny])
            aI[z, :nx, :ny] = heat_side * harmonic(mid, pltpu.roll(kap, 1, 0)[:nx, :ny])
            aI[z, :nx, ny:] = heat_side * harmonic(mid, pltpu.roll(kap, COLS - 1, 1)[:nx, :ny])
            rI[z, :nx, :ny] = heat_side * harmonic(mid, pltpu.roll(kap, 1, 1)[:nx, :ny])
            has = jnp.where(z < nz - 1, heat_vert, 0.0)
            rI[z, :nx, ny:] = has * harmonic(mid, kb[z + 2, :nx, :ny])
            return carry

        levels(second, 0)
        sI[0, :nx, :ny] = sI[0, :nx, :ny] + 2.0 * heat_vert * kb[1, :nx, :ny] * surface[...]

    def heat_solve(dst):
        def forward(z, carry):
            above, ratio, value = carry
            x = xw[z]
            t = x[:nx, :ny]
            cap, lm = bI[z, :nx, :ny], bI[z, :nx, ny:]
            f = sigmoid2(t)
            apparent = cap + lm * f * (1.0 - f) * 2.0
            lateral = sI[z, :nx, ny:] * (pltpu.roll(x, ROWS - 1, 0)[:nx, :ny] - t)
            lateral += aI[z, :nx, :ny] * (pltpu.roll(x, 1, 0)[:nx, :ny] - t)
            lateral += aI[z, :nx, ny:] * (pltpu.roll(x, COLS - 1, 1)[:nx, :ny] - t)
            lateral += rI[z, :nx, :ny] * (pltpu.roll(x, 1, 1)[:nx, :ny] - t)
            right = apparent * t - (cap * t + lm * f) + sI[z, :nx, :ny] + lateral
            below = rI[z, :nx, ny:]
            inv = 1.0 / (apparent + above + below + above * ratio)
            ratio = -below * inv
            value = (right + above * value) * inv
            vb[z, :nx, :ny] = value
            vb[z, :nx, ny:] = ratio
            return (below, ratio, value)

        zero = jnp.zeros((nx, ny), jnp.float32)
        levels(forward, (2.0 * heat_vert * kb[1, :nx, :ny], zero, zero))

        def backward(z, lower):
            solved = vb[z, :nx, :ny] - vb[z, :nx, ny:] * lower
            dst[z] = solved
            return solved

        levels(backward, zero, down=False)

    def flow_setup():
        kb[0] = one
        kb[nz + 1] = one

        def first(z, carry):
            temper, head, kind = wide(*oth, z), wide(*own, z), wide(soil, soil_rc, soil_c, z)
            look = looker(kind)
            liquid, alpha, poro, suction, satur = state(temper, head, look)
            cube = satur * satur * satur
            kb[z + 1] = look(3) * cube * jnp.exp(-2.0 * (1.0 - liquid))
            vb[z] = storage + poro * 0.9 * alpha * alpha * suction * cube
            xw[z] = head
            return carry

        levels(first, 0)

        def second(z, carry):
            above, ratio = carry
            hyd, cap, x = kb[z + 1], vb[z], xw[z]
            has = jnp.where(z < nz - 1, flow_vert * 0.5, 0.0)
            drain = jnp.where(z < nz - 1, 0.0, elevation)
            below = has * (hyd + kb[z + 2])
            side = flow_side * hyd
            inv = 1.0 / (cap + above + below + 4.0 * side - above * ratio)
            ratio = below * inv
            base = cap * x + elevation * (above - below) - drain * hyd
            bI[z] = jnp.where(free, base * inv, x)
            sI[z] = jnp.where(free, side * inv, 0.0)
            aI[z] = jnp.where(free, above * inv, 0.0)
            rI[z] = jnp.where(free, ratio, 0.0)
            return (below, ratio)

        zero = jnp.zeros((ROWS, COLS), jnp.float32)
        levels(second, (zero, zero))

    def flow_solve(dst):
        for inner in range(INNER):
            last = inner == INNER - 1
            h, w = (nx, ny) if last else (ROWS, COLS)

            def forward(z, value):
                x = xw[z]
                near = pltpu.roll(x, 1, 0) + pltpu.roll(x, ROWS - 1, 0)
                near = near[:h, :w] + (pltpu.roll(x, 1, 1) + pltpu.roll(x, COLS - 1, 1))[:h, :w]
                value = bI[z, :h, :w] + sI[z, :h, :w] * near + aI[z, :h, :w] * value
                vb[z, :h, :w] = value
                return value

            zero = jnp.zeros((h, w), jnp.float32)
            levels(forward, zero)

            def backward(z, lower):
                solved = vb[z, :h, :w] + rI[z, :h, :w] * lower
                if last:
                    dst[z] = solved
                else:
                    xw[z] = solved
                return solved

            levels(backward, zero, down=False)

    @pl.when(is_heat)
    def _():
        heat_setup()
        heat_solve(res)

    @pl.when(jnp.logical_not(is_heat))
    def _():
        flow_setup()
        flow_solve(res)

    it_wait = edges(res, it_rc, it_cs, it_c, 2)
    it_wait()

    @pl.when(is_heat)
    def _():
        def fill(z, carry):
            xw[z] = wide(res, it_rc, it_c, z)
            return carry

        levels(fill, 0)
        heat_solve(res2)

    @pl.when(jnp.logical_not(is_heat))
    def _():
        def fill(z, carry):
            x = wide(res, it_rc, it_c, z)
            xw[z] = x
            bI[z] = jnp.where(free, bI[z], x)
            return carry

        levels(fill, 0)
        flow_solve(res2)

    lanes = pl.ds(pl.multiple_of(c * ny, ny), ny)
    moves = []
    for k in range(1, n_col):
        to = lax.rem(c + k, n_col)
        moves.append(
            remote(res2.at[pl.ds(to * zs, zs)], out.at[0, :, :, lanes], fin_s.at[k - 1], fin_r.at[k - 1], col=to)
        )
    local = pltpu.make_async_copy(res2.at[pl.ds(c * zs, zs)], out.at[0, :, :, lanes], loc_sem.at[1])
    for move in moves:
        move.start()
    local.start()
    local.wait()
    for move in moves:
        move.wait()


def solution(mesh):
    n_grp, n_col = mesh.shape["grp"], mesh.shape["col"]

    def on_device(fields, soil_type, surface, heat_cond, heat_capacity, porosity, sat_cond, vg_alpha):
        nz, nx, ny = soil_type.shape
        f32, i32 = jnp.float32, jnp.int32
        whole = lambda t: pltpu.VMEM((nz, nx, ny), t)
        tile = lambda t: pltpu.VMEM((nz, 8, ny), t)
        strip = lambda t: pltpu.VMEM((2, ROWS, ny), t)
        field = pltpu.VMEM((nz, ROWS, COLS), f32)
        dma = lambda *s: pltpu.SemaphoreType.DMA(s)
        part = pltpu.VMEM((2, nx, ny), f32)
        scratch = [
            whole(i32), pltpu.VMEM((nx, ny), f32), pltpu.SMEM((5, heat_cond.shape[0]), f32),
            whole(f32), whole(f32), tile(f32), tile(f32), part, strip(f32), strip(f32),
            tile(i32), pltpu.VMEM((2, nx, ny), i32), strip(i32),
            whole(f32), tile(f32), part, strip(f32), whole(f32),
            field, field, field, field, field, field, pltpu.VMEM((nz + 2, ROWS, COLS), f32),
            dma(9), dma(n_col - 1), dma(n_col - 1), dma(n_col + 2), dma(n_col + 2), dma(3, 8), dma(3, 8),
            dma(n_col - 1), dma(n_col - 1),
        ]
        anywhere = pl.BlockSpec(memory_space=pl.ANY)
        return pl.pallas_call(
            functools.partial(kernel, n_grp, n_col),
            out_shape=jax.ShapeDtypeStruct(fields.shape, f32),
            in_specs=[anywhere] * 8,
            out_specs=anywhere,
            scratch_shapes=scratch,
            compiler_params=pltpu.CompilerParams(
                collective_id=0, has_side_effects=True, vmem_limit_bytes=58 * 2**20
            ),
            name="step",
        )(fields, soil_type, surface, heat_cond, heat_capacity, porosity, sat_cond, vg_alpha)

    in_specs = (
        P("sec", "col", "grp", None), P(None, "grp", "col"), P("grp", "col"),
        P(), P(), P(), P(), P(),
    )
    return jax.shard_map(
        on_device, mesh=mesh, in_specs=in_specs, out_specs=P("sec", "col", "grp", None), check_vma=False
    )
```

```python
import functools
import jax
import jax.numpy as jnp
from jax import lax
from jax.experimental import pallas as pl
from jax.experimental.pallas import tpu as pltpu
from jax.sharding import PartitionSpec as P

OUTER = 2
INNER = 3
CHUNK = 16
ROWS = 40
COLS = 256
MESH = pl.DeviceIdType.MESH

heat_side = 0.2
heat_vert = 8.0
storage = 0.001
flow_side = 0.002
flow_vert = 1.5
elevation = 0.1


def harmonic(a, b):
    return 2.0 * a * b / (a + b)


def sigmoid2(x):
    return 1.0 / (1.0 + jnp.exp(-2.0 * x))


def kernel(
    n_grp, n_col, fields, soil_in, surface_in, tab_0, tab_1, tab_2, tab_3, tab_4, out,
    soil, surface, tab,
    own_m, oth_m, own_rc, oth_rc, own_cs, own_c, oth_c,
    soil_rc, soil_cs, soil_c,
    res, it_rc, it_cs, it_c, res2,
    xw, vb, bI, sI, aI, rI, kb,
    loc_sem, a2a_s, a2a_r, sec_s, sec_r, edge_s, edge_r, fin_s, fin_r,
):
    sec = lax.axis_index("sec")
    g = lax.axis_index("grp")
    c = lax.axis_index("col")
    nz, nx, ny = soil.shape
    zs = fields.shape[1]
    is_heat = sec == 0

    def inside(dg, dc):
        ok = None
        for at, d, count in ((g, dg, n_grp), (c, dc, n_col)):
            if d:
                here = at < count - 1 if d > 0 else at > 0
                ok = here if ok is None else jnp.logical_and(ok, here)
        return ok

    way = [(1, 0), (-1, 0), (0, 1), (0, -1), (1, 1), (-1, 1), (1, -1), (-1, -1)]

    def at_way(dg, dc):
        return {"grp": lax.rem(g + dg + n_grp, n_grp), "col": lax.rem(c + dc + n_col, n_col)}

    barrier = pltpu.get_barrier_semaphore()
    for buffer in (own_rc, soil_rc, it_rc, own_c, soil_c, it_c):
        buffer[...] = jnp.zeros(buffer.shape, buffer.dtype)
    met = n_col
    for k in range(1, n_col):
        pl.semaphore_signal(barrier, inc=1, device_id={"col": lax.rem(c + k, n_col)}, device_id_type=MESH)
    pl.semaphore_signal(barrier, inc=1, device_id={"sec": 1 - sec}, device_id_type=MESH)
    for dg, dc in way:
        if dg:
            met = met + jnp.where(inside(dg, dc), 1, 0)

            @pl.when(inside(dg, dc))
            def _():
                pl.semaphore_signal(barrier, inc=1, device_id=at_way(dg, dc), device_id_type=MESH)

    pl.semaphore_wait(barrier, met)

    def remote(src, dst, s, r, **where):
        return pltpu.make_async_remote_copy(
            src_ref=src, dst_ref=dst, send_sem=s, recv_sem=r, device_id=where, device_id_type=MESH
        )

    def edges(m, rc, cs, cc, slot):
        low, high = pl.ds(0, 2), pl.ds(nx - 2, 2)
        above, below = pl.ds(ROWS - 2, 2), pl.ds(nx, 2)
        parts = [
            (m.at[:, high, :], rc.at[:, pl.ds(6, 2), :]),
            (m.at[:, low, :], rc.at[:, pl.ds(0, 2), :]),
            (cs.at[0], cc.at[0, pl.ds(0, nx), :]),
            (cs.at[1], cc.at[1, pl.ds(0, nx), :]),
            (cs.at[0, high, :], cc.at[0, above, :]),
            (cs.at[0, low, :], cc.at[0, below, :]),
            (cs.at[1, high, :], cc.at[1, above, :]),
            (cs.at[1, low, :], cc.at[1, below, :]),
        ]
        copies = [
            remote(src, dst, edge_s.at[slot, i], edge_r.at[slot, i], **at_way(*way[i]))
            for i, (src, dst) in enumerate(parts)
        ]

        def start(these):
            for i in these:
                @pl.when(inside(*way[i]))
                def _():
                    copies[i].start()

        start((0, 1))
        pack(m, cs)
        start(range(2, 8))

        def wait():
            for i, (dg, dc) in enumerate(way):
                @pl.when(inside(dg, dc))
                def _():
                    copies[i].wait_send()

                @pl.when(inside(-dg, -dc))
                def _():
                    copies[i].wait_recv()

        return wait

    lane = lax.broadcasted_iota(jnp.int32, (ROWS, ny), 1)

    def levels(body, carry, down=True):
        def chunk(i, carry):
            for u in range(CHUNK):
                step = i * CHUNK + u
                carry = body(step if down else nz - 1 - step, carry)
            return carry

        return lax.fori_loop(0, nz // CHUNK, chunk, carry)

    def pack(m, cs):
        pair = lax.shift_right_logical(lax.broadcasted_iota(jnp.int32, (nx, ny), 1), 1)

        def body(z, carry):
            ahead, back = carry
            plane = m[z]
            ahead = jnp.where(pair == z, pltpu.roll(plane, lax.rem(2 * z + 2, ny), 1), ahead)
            back = jnp.where(pair == z, pltpu.roll(plane, 2 * z, 1), back)
            return (ahead, back)

        zero = jnp.zeros((nx, ny), m.dtype)
        ahead, back = levels(body, (zero, zero))
        cs[0] = ahead
        cs[1] = back

    def wide(m, rc, cc, z):
        tile = jnp.concatenate([m[z], rc[z]], axis=0)
        right = pltpu.roll(cc[1], lax.rem(ny - 2 * z, ny), 1)
        left = pltpu.roll(cc[0], ny - 2 - 2 * z, 1)
        return jnp.concatenate([tile, jnp.where(lane < 64, right, left)], axis=1)

    tabs = (tab_0, tab_1, tab_2, tab_3, tab_4)
    loads = [pltpu.make_async_copy(soil_in, soil, loc_sem.at[2]), pltpu.make_async_copy(surface_in, surface, loc_sem.at[3])]
    loads += [pltpu.make_async_copy(t, tab.at[i], loc_sem.at[4 + i]) for i, t in enumerate(tabs)]
    local = pltpu.make_async_copy(
        fields.at[0, :, :, pl.ds(pl.multiple_of(c * ny, ny), ny)], own_m.at[pl.ds(c * zs, zs)], loc_sem.at[0]
    )
    moves = []
    for k in range(1, n_col):
        to = lax.rem(c + k, n_col)
        moves.append(
            remote(
                fields.at[0, :, :, pl.ds(pl.multiple_of(to * ny, ny), ny)],
                own_m.at[pl.ds(c * zs, zs)],
                a2a_s.at[k - 1], a2a_r.at[k - 1], col=to,
            )
        )
    for move in moves:
        move.start()
    local.start()
    for load in loads:
        load.start()
    loads[0].wait()
    soil_wait = edges(soil, soil_rc, soil_cs, soil_c, 0)

    other = 1 - sec
    swaps = []

    def swap(src, dst):
        i = len(swaps)
        swaps.append(remote(src, dst, sec_s.at[i], sec_r.at[i], sec=other))
        swaps[i].start()

    local.wait()
    swap(own_m.at[pl.ds(c * zs, zs)], oth_m.at[pl.ds(c * zs, zs)])
    for k, move in enumerate(moves):
        move.wait_recv()
        came = lax.rem(c + n_col - 1 - k, n_col)
        swap(own_m.at[pl.ds(came * zs, zs)], oth_m.at[pl.ds(came * zs, zs)])
    own_wait = edges(own_m, own_rc, own_cs, own_c, 1)
    own_wait()
    swap(own_rc, oth_rc)
    swap(own_c, oth_c)
    for move in moves:
        move.wait_send()
    soil_wait()
    for load in loads[1:]:
        load.wait()
    for one_swap in swaps:
        one_swap.wait()

    own = (own_m, own_rc, own_c)
    oth = (oth_m, oth_rc, oth_c)

    def looker(kind):
        b0, b1, b2 = (kind & 1) != 0, (kind & 2) != 0, (kind & 4) != 0

        def look(row):
            t = [tab[row, i] for i in range(8)]
            q = [jnp.where(b0, t[2 * i + 1], t[2 * i]) for i in range(4)]
            return jnp.where(b2, jnp.where(b1, q[3], q[2]), jnp.where(b1, q[1], q[0]))

        return look

    def state(temper, head, look):
        liquid = sigmoid2(temper)
        alpha, poro = look(4), look(2)
        suction = jnp.maximum(-head, 0.0)
        a_s = alpha * suction
        satur = lax.rsqrt(1.0 + a_s * a_s)
        return liquid, alpha, poro, suction, satur

    one = jnp.ones((ROWS, COLS), jnp.float32)
    row_i = lax.broadcasted_iota(jnp.int32, (ROWS, COLS), 0)
    col_i = lax.broadcasted_iota(jnp.int32, (ROWS, COLS), 1)
    free = ((row_i <= nx) | (row_i == ROWS - 1)) & ((col_i <= ny) | (col_i == COLS - 1))

    def heat_setup():
        kb[0] = one
        kb[nz + 1] = one

        def first(z, carry):
            temper, head, kind = wide(*own, z), wide(*oth, z), wide(soil, soil_rc, soil_c, z)
            look = looker(kind)
            liquid, alpha, poro, suction, satur = state(temper, head, look)
            moist = poro * (0.1 + 0.9 * satur)
            kb[z + 1] = look(0) * (1.0 + moist * (1.0 - liquid))
            xw[z] = temper
            cap = looker(soil[z])(1)
            lm = 4.0 * moist[:nx, :ny]
            bI[z, :nx, :ny] = cap
            bI[z, :nx, ny:] = lm
            sI[z, :nx, :ny] = cap * temper[:nx, :ny] + lm * liquid[:nx, :ny]
            return carry

        levels(first, 0)

        def second(z, carry):
            kap = kb[z + 1]
            mid = kap[:nx, :ny]
            sI[z, :nx, ny:] = heat_side * harmonic(mid, pltpu.roll(kap, ROWS - 1, 0)[:nx, :ny])
            aI[z, :nx, :ny] = heat_side * harmonic(mid, pltpu.roll(kap, 1, 0)[:nx, :ny])
            aI[z, :nx, ny:] = heat_side * harmonic(mid, pltpu.roll(kap, COLS - 1, 1)[:nx, :ny])
            rI[z, :nx, :ny] = heat_side * harmonic(mid, pltpu.roll(kap, 1, 1)[:nx, :ny])
            has = jnp.where(z < nz - 1, heat_vert, 0.0)
            rI[z, :nx, ny:] = has * harmonic(mid, kb[z + 2, :nx, :ny])
            return carry

        levels(second, 0)
        sI[0, :nx, :ny] = sI[0, :nx, :ny] + 2.0 * heat_vert * kb[1, :nx, :ny] * surface[...]

    def heat_solve(dst):
        def forward(z, carry):
            above, ratio, value = carry
            x = xw[z]
            t = x[:nx, :ny]
            cap, lm = bI[z, :nx, :ny], bI[z, :nx, ny:]
            f = sigmoid2(t)
            apparent = cap + lm * f * (1.0 - f) * 2.0
            lateral = sI[z, :nx, ny:] * (pltpu.roll(x, ROWS - 1, 0)[:nx, :ny] - t)
            lateral += aI[z, :nx, :ny] * (pltpu.roll(x, 1, 0)[:nx, :ny] - t)
            lateral += aI[z, :nx, ny:] * (pltpu.roll(x, COLS - 1, 1)[:nx, :ny] - t)
            lateral += rI[z, :nx, :ny] * (pltpu.roll(x, 1, 1)[:nx, :ny] - t)
            right = apparent * t - (cap * t + lm * f) + sI[z, :nx, :ny] + lateral
            below = rI[z, :nx, ny:]
            inv = 1.0 / (apparent + above + below + above * ratio)
            ratio = -below * inv
            value = (right + above * value) * inv
            vb[z, :nx, :ny] = value
            vb[z, :nx, ny:] = ratio
            return (below, ratio, value)

        zero = jnp.zeros((nx, ny), jnp.float32)
        levels(forward, (2.0 * heat_vert * kb[1, :nx, :ny], zero, zero))

        def backward(z, lower):
            solved = vb[z, :nx, :ny] - vb[z, :nx, ny:] * lower
            dst[z] = solved
            return solved

        levels(backward, zero, down=False)

    def flow_setup():
        kb[0] = one
        kb[nz + 1] = one

        def first(z, carry):
            temper, head, kind = wide(*oth, z), wide(*own, z), wide(soil, soil_rc, soil_c, z)
            look = looker(kind)
            liquid, alpha, poro, suction, satur = state(temper, head, look)
            cube = satur * satur * satur
            kb[z + 1] = look(3) * cube * jnp.exp(-2.0 * (1.0 - liquid))
            vb[z] = storage + poro * 0.9 * alpha * alpha * suction * cube
            xw[z] = head
            return carry

        levels(first, 0)

        def second(z, carry):
            above, ratio = carry
            hyd, cap, x = kb[z + 1], vb[z], xw[z]
            has = jnp.where(z < nz - 1, flow_vert * 0.5, 0.0)
            drain = jnp.where(z < nz - 1, 0.0, elevation)
            below = has * (hyd + kb[z + 2])
            side = flow_side * hyd
            inv = 1.0 / (cap + above + below + 4.0 * side - above * ratio)
            ratio = below * inv
            base = cap * x + elevation * (above - below) - drain * hyd
            bI[z] = jnp.where(free, base * inv, x)
            sI[z] = jnp.where(free, side * inv, 0.0)
            aI[z] = jnp.where(free, above * inv, 0.0)
            rI[z] = jnp.where(free, ratio, 0.0)
            return (below, ratio)

        zero = jnp.zeros((ROWS, COLS), jnp.float32)
        levels(second, (zero, zero))

    def flow_solve(dst):
        for inner in range(INNER):
            last = inner == INNER - 1
            h, w = (nx, ny) if last else (ROWS, COLS)

            def forward(z, value):
                x = xw[z]
                near = pltpu.roll(x, 1, 0) + pltpu.roll(x, ROWS - 1, 0)
                near = near[:h, :w] + (pltpu.roll(x, 1, 1) + pltpu.roll(x, COLS - 1, 1))[:h, :w]
                value = bI[z, :h, :w] + sI[z, :h, :w] * near + aI[z, :h, :w] * value
                vb[z, :h, :w] = value
                return value

            zero = jnp.zeros((h, w), jnp.float32)
            levels(forward, zero)

            def backward(z, lower):
                solved = vb[z, :h, :w] + rI[z, :h, :w] * lower
                if last:
                    dst[z] = solved
                else:
                    xw[z] = solved
                return solved

            levels(backward, zero, down=False)

    @pl.when(is_heat)
    def _():
        heat_setup()
        heat_solve(res)

    @pl.when(jnp.logical_not(is_heat))
    def _():
        flow_setup()
        flow_solve(res)

    it_wait = edges(res, it_rc, it_cs, it_c, 2)
    it_wait()

    @pl.when(is_heat)
    def _():
        def fill(z, carry):
            xw[z] = wide(res, it_rc, it_c, z)
            return carry

        levels(fill, 0)
        heat_solve(res2)

    @pl.when(jnp.logical_not(is_heat))
    def _():
        def fill(z, carry):
            x = wide(res, it_rc, it_c, z)
            xw[z] = x
            bI[z] = jnp.where(free, bI[z], x)
            return carry

        levels(fill, 0)
        flow_solve(res2)

    lanes = pl.ds(pl.multiple_of(c * ny, ny), ny)
    moves = []
    for k in range(1, n_col):
        to = lax.rem(c + k, n_col)
        moves.append(
            remote(res2.at[pl.ds(to * zs, zs)], out.at[0, :, :, lanes], fin_s.at[k - 1], fin_r.at[k - 1], col=to)
        )
    local = pltpu.make_async_copy(res2.at[pl.ds(c * zs, zs)], out.at[0, :, :, lanes], loc_sem.at[1])
    for move in moves:
        move.start()
    local.start()
    local.wait()
    for move in moves:
        move.wait()


def solution(mesh):
    n_grp, n_col = mesh.shape["grp"], mesh.shape["col"]

    def on_device(fields, soil_type, surface, heat_cond, heat_capacity, porosity, sat_cond, vg_alpha):
        nz, nx, ny = soil_type.shape
        f32, i32 = jnp.float32, jnp.int32
        whole = lambda t: pltpu.VMEM((nz, nx, ny), t)
        tile = lambda t: pltpu.VMEM((nz, 8, ny), t)
        strip = lambda t: pltpu.VMEM((2, ROWS, ny), t)
        field = pltpu.VMEM((nz, ROWS, COLS), f32)
        dma = lambda *s: pltpu.SemaphoreType.DMA(s)
        part = pltpu.VMEM((2, nx, ny), f32)
        scratch = [
            whole(i32), pltpu.VMEM((nx, ny), f32), pltpu.SMEM((5, heat_cond.shape[0]), f32),
            whole(f32), whole(f32), tile(f32), tile(f32), part, strip(f32), strip(f32),
            tile(i32), pltpu.VMEM((2, nx, ny), i32), strip(i32),
            whole(f32), tile(f32), part, strip(f32), whole(f32),
            field, field, field, field, field, field, pltpu.VMEM((nz + 2, ROWS, COLS), f32),
            dma(9), dma(n_col - 1), dma(n_col - 1), dma(n_col + 2), dma(n_col + 2), dma(3, 8), dma(3, 8),
            dma(n_col - 1), dma(n_col - 1),
        ]
        anywhere = pl.BlockSpec(memory_space=pl.ANY)
        return pl.pallas_call(
            functools.partial(kernel, n_grp, n_col),
            out_shape=jax.ShapeDtypeStruct(fields.shape, f32),
            in_specs=[anywhere] * 8,
            out_specs=anywhere,
            scratch_shapes=scratch,
            compiler_params=pltpu.CompilerParams(
                collective_id=0, has_side_effects=True, vmem_limit_bytes=58 * 2**20
            ),
            name="step",
        )(fields, soil_type, surface, heat_cond, heat_capacity, porosity, sat_cond, vg_alpha)

    in_specs = (
        P("sec", "col", "grp", None), P(None, "grp", "col"), P("grp", "col"),
        P(), P(), P(), P(), P(),
    )
    return jax.shard_map(
        on_device, mesh=mesh, in_specs=in_specs, out_specs=P("sec", "col", "grp", None), check_vma=False
    )
```

```python
import functools
import jax
import jax.numpy as jnp
from jax import lax
from jax.experimental import pallas as pl
from jax.experimental.pallas import tpu as pltpu
from jax.sharding import PartitionSpec as P

OUTER = 2
INNER = 3
CHUNK = 16
ROWS = 40
COLS = 256
MESH = pl.DeviceIdType.MESH

heat_side = 0.2
heat_vert = 8.0
storage = 0.001
flow_side = 0.002
flow_vert = 1.5
elevation = 0.1


def harmonic(a, b):
    return 2.0 * a * b / (a + b)


def sigmoid2(x):
    return 1.0 / (1.0 + jnp.exp(-2.0 * x))


def kernel(
    n_grp, n_col, fields, soil_in, surface_in, tab_0, tab_1, tab_2, tab_3, tab_4, out,
    soil, surface, tab,
    own_m, oth_m, own_rc, oth_rc, own_cs, own_c, oth_c,
    soil_rc, soil_cs, soil_c,
    res, it_rc, it_cs, it_c, res2,
    xw, vb, bI, sI, aI, rI, kb,
    loc_sem, a2a_s, a2a_r, sec_s, sec_r, edge_s, edge_r, fin_s, fin_r,
):
    sec = lax.axis_index("sec")
    g = lax.axis_index("grp")
    c = lax.axis_index("col")
    nz, nx, ny = soil.shape
    zs = fields.shape[1]
    is_heat = sec == 0

    def inside(dg, dc):
        ok = None
        for at, d, count in ((g, dg, n_grp), (c, dc, n_col)):
            if d:
                here = at < count - 1 if d > 0 else at > 0
                ok = here if ok is None else jnp.logical_and(ok, here)
        return ok

    way = [(1, 0), (-1, 0), (0, 1), (0, -1), (1, 1), (-1, 1), (1, -1), (-1, -1)]

    def at_way(dg, dc):
        return {"grp": lax.rem(g + dg + n_grp, n_grp), "col": lax.rem(c + dc + n_col, n_col)}

    barrier = pltpu.get_barrier_semaphore()
    for buffer in (own_rc, soil_rc, it_rc, own_c, soil_c, it_c):
        buffer[...] = jnp.zeros(buffer.shape, buffer.dtype)
    met = n_col
    for k in range(1, n_col):
        pl.semaphore_signal(barrier, inc=1, device_id={"col": lax.rem(c + k, n_col)}, device_id_type=MESH)
    pl.semaphore_signal(barrier, inc=1, device_id={"sec": 1 - sec}, device_id_type=MESH)
    for dg, dc in way:
        if dg:
            met = met + jnp.where(inside(dg, dc), 1, 0)

            @pl.when(inside(dg, dc))
            def _():
                pl.semaphore_signal(barrier, inc=1, device_id=at_way(dg, dc), device_id_type=MESH)

    pl.semaphore_wait(barrier, met)

    def remote(src, dst, s, r, **where):
        return pltpu.make_async_remote_copy(
            src_ref=src, dst_ref=dst, send_sem=s, recv_sem=r, device_id=where, device_id_type=MESH
        )

    def edges(m, rc, cs, cc, slot):
        low, high = pl.ds(0, 2), pl.ds(nx - 2, 2)
        above, below = pl.ds(ROWS - 2, 2), pl.ds(nx, 2)
        parts = [
            (m.at[:, high, :], rc.at[:, pl.ds(6, 2), :]),
            (m.at[:, low, :], rc.at[:, pl.ds(0, 2), :]),
            (cs.at[0], cc.at[0, pl.ds(0, nx), :]),
            (cs.at[1], cc.at[1, pl.ds(0, nx), :]),
            (cs.at[0, high, :], cc.at[0, above, :]),
            (cs.at[0, low, :], cc.at[0, below, :]),
            (cs.at[1, high, :], cc.at[1, above, :]),
            (cs.at[1, low, :], cc.at[1, below, :]),
        ]
        copies = [
            remote(src, dst, edge_s.at[slot, i], edge_r.at[slot, i], **at_way(*way[i]))
            for i, (src, dst) in enumerate(parts)
        ]

        def start(these):
            for i in these:
                @pl.when(inside(*way[i]))
                def _():
                    copies[i].start()

        start(range(8))

        def wait():
            for i, (dg, dc) in enumerate(way):
                @pl.when(inside(dg, dc))
                def _():
                    copies[i].wait_send()

                @pl.when(inside(-dg, -dc))
                def _():
                    copies[i].wait_recv()

        return wait

    lane = lax.broadcasted_iota(jnp.int32, (ROWS, ny), 1)

    def levels(body, carry, down=True):
        def chunk(i, carry):
            for u in range(CHUNK):
                step = i * CHUNK + u
                carry = body(step if down else nz - 1 - step, carry)
            return carry

        return lax.fori_loop(0, nz // CHUNK, chunk, carry)

    pair = lax.shift_right_logical(lax.broadcasted_iota(jnp.int32, (nx, ny), 1), 1)

    def packed(z, plane, strips):
        ahead, back = strips
        ahead = jnp.where(pair == z, pltpu.roll(plane, lax.rem(2 * z + 2, ny), 1), ahead)
        back = jnp.where(pair == z, pltpu.roll(plane, 2 * z, 1), back)
        return (ahead, back)

    def no_strips(dtype):
        zero = jnp.zeros((nx, ny), dtype)
        return (zero, zero)

    def pack_slab(m, slab, strips):
        for u in range(zs):
            strips = packed(slab * zs + u, m[slab * zs + u], strips)
        return strips

    def keep(cs, strips):
        cs[0] = strips[0]
        cs[1] = strips[1]

    def wide(m, rc, cc, z):
        tile = jnp.concatenate([m[z], rc[z]], axis=0)
        right = pltpu.roll(cc[1], lax.rem(ny - 2 * z, ny), 1)
        left = pltpu.roll(cc[0], ny - 2 - 2 * z, 1)
        return jnp.concatenate([tile, jnp.where(lane < 64, right, left)], axis=1)

    tabs = (tab_0, tab_1, tab_2, tab_3, tab_4)
    loads = [pltpu.make_async_copy(soil_in, soil, loc_sem.at[2]), pltpu.make_async_copy(surface_in, surface, loc_sem.at[3])]
    loads += [pltpu.make_async_copy(t, tab.at[i], loc_sem.at[4 + i]) for i, t in enumerate(tabs)]
    local = pltpu.make_async_copy(
        fields.at[0, :, :, pl.ds(pl.multiple_of(c * ny, ny), ny)], own_m.at[pl.ds(c * zs, zs)], loc_sem.at[0]
    )
    moves = []
    for k in range(1, n_col):
        to = lax.rem(c + k, n_col)
        moves.append(
            remote(
                fields.at[0, :, :, pl.ds(pl.multiple_of(to * ny, ny), ny)],
                own_m.at[pl.ds(c * zs, zs)],
                a2a_s.at[k - 1], a2a_r.at[k - 1], col=to,
            )
        )
    for move in moves:
        move.start()
    local.start()
    for load in loads:
        load.start()
    loads[0].wait()
    keep(soil_cs, levels(lambda z, strips: packed(z, soil[z], strips), no_strips(soil.dtype)))
    soil_wait = edges(soil, soil_rc, soil_cs, soil_c, 0)

    other = 1 - sec
    swaps = []

    def swap(src, dst):
        i = len(swaps)
        swaps.append(remote(src, dst, sec_s.at[i], sec_r.at[i], sec=other))
        swaps[i].start()

    local.wait()
    swap(own_m.at[pl.ds(c * zs, zs)], oth_m.at[pl.ds(c * zs, zs)])
    strips = pack_slab(own_m, c, no_strips(own_m.dtype))
    for k, move in enumerate(moves):
        move.wait_recv()
        came = lax.rem(c + n_col - 1 - k, n_col)
        swap(own_m.at[pl.ds(came * zs, zs)], oth_m.at[pl.ds(came * zs, zs)])
        strips = pack_slab(own_m, came, strips)
    keep(own_cs, strips)
    own_wait = edges(own_m, own_rc, own_cs, own_c, 1)
    own_wait()
    swap(own_rc, oth_rc)
    swap(own_c, oth_c)
    for move in moves:
        move.wait_send()
    soil_wait()
    for load in loads[1:]:
        load.wait()
    for one_swap in swaps:
        one_swap.wait()

    own = (own_m, own_rc, own_c)
    oth = (oth_m, oth_rc, oth_c)

    def looker(kind):
        b0, b1, b2 = (kind & 1) != 0, (kind & 2) != 0, (kind & 4) != 0

        def look(row):
            t = [tab[row, i] for i in range(8)]
            q = [jnp.where(b0, t[2 * i + 1], t[2 * i]) for i in range(4)]
            return jnp.where(b2, jnp.where(b1, q[3], q[2]), jnp.where(b1, q[1], q[0]))

        return look

    def state(temper, head, look):
        liquid = sigmoid2(temper)
        alpha, poro = look(4), look(2)
        suction = jnp.maximum(-head, 0.0)
        a_s = alpha * suction
        satur = lax.rsqrt(1.0 + a_s * a_s)
        return liquid, alpha, poro, suction, satur

    one = jnp.ones((ROWS, COLS), jnp.float32)
    row_i = lax.broadcasted_iota(jnp.int32, (ROWS, COLS), 0)
    col_i = lax.broadcasted_iota(jnp.int32, (ROWS, COLS), 1)
    free = ((row_i <= nx) | (row_i == ROWS - 1)) & ((col_i <= ny) | (col_i == COLS - 1))

    def heat_setup():
        kb[0] = one
        kb[nz + 1] = one

        def first(z, carry):
            temper, head, kind = wide(*own, z), wide(*oth, z), wide(soil, soil_rc, soil_c, z)
            look = looker(kind)
            liquid, alpha, poro, suction, satur = state(temper, head, look)
            moist = poro * (0.1 + 0.9 * satur)
            kb[z + 1] = look(0) * (1.0 + moist * (1.0 - liquid))
            xw[z] = temper
            cap = looker(soil[z])(1)
            lm = 4.0 * moist[:nx, :ny]
            bI[z, :nx, :ny] = cap
            bI[z, :nx, ny:] = lm
            sI[z, :nx, :ny] = cap * temper[:nx, :ny] + lm * liquid[:nx, :ny]
            return carry

        levels(first, 0)

        def second(z, carry):
            kap = kb[z + 1]
            mid = kap[:nx, :ny]
            sI[z, :nx, ny:] = heat_side * harmonic(mid, pltpu.roll(kap, ROWS - 1, 0)[:nx, :ny])
            aI[z, :nx, :ny] = heat_side * harmonic(mid, pltpu.roll(kap, 1, 0)[:nx, :ny])
            aI[z, :nx, ny:] = heat_side * harmonic(mid, pltpu.roll(kap, COLS - 1, 1)[:nx, :ny])
            rI[z, :nx, :ny] = heat_side * harmonic(mid, pltpu.roll(kap, 1, 1)[:nx, :ny])
            has = jnp.where(z < nz - 1, heat_vert, 0.0)
            rI[z, :nx, ny:] = has * harmonic(mid, kb[z + 2, :nx, :ny])
            return carry

        levels(second, 0)
        sI[0, :nx, :ny] = sI[0, :nx, :ny] + 2.0 * heat_vert * kb[1, :nx, :ny] * surface[...]

    def heat_solve(dst, strip=None):
        def forward(z, carry):
            above, ratio, value = carry
            x = xw[z]
            t = x[:nx, :ny]
            cap, lm = bI[z, :nx, :ny], bI[z, :nx, ny:]
            f = sigmoid2(t)
            apparent = cap + lm * f * (1.0 - f) * 2.0
            lateral = sI[z, :nx, ny:] * (pltpu.roll(x, ROWS - 1, 0)[:nx, :ny] - t)
            lateral += aI[z, :nx, :ny] * (pltpu.roll(x, 1, 0)[:nx, :ny] - t)
            lateral += aI[z, :nx, ny:] * (pltpu.roll(x, COLS - 1, 1)[:nx, :ny] - t)
            lateral += rI[z, :nx, :ny] * (pltpu.roll(x, 1, 1)[:nx, :ny] - t)
            right = apparent * t - (cap * t + lm * f) + sI[z, :nx, :ny] + lateral
            below = rI[z, :nx, ny:]
            inv = 1.0 / (apparent + above + below + above * ratio)
            ratio = -below * inv
            value = (right + above * value) * inv
            vb[z, :nx, :ny] = value
            vb[z, :nx, ny:] = ratio
            return (below, ratio, value)

        zero = jnp.zeros((nx, ny), jnp.float32)
        levels(forward, (2.0 * heat_vert * kb[1, :nx, :ny], zero, zero))

        def backward(z, carry):
            lower, strips = carry
            solved = vb[z, :nx, :ny] - vb[z, :nx, ny:] * lower
            dst[z] = solved
            return (solved, packed(z, solved, strips) if strip is not None else strips)

        unused, strips = levels(backward, (zero, no_strips(zero.dtype)), down=False)
        if strip is not None:
            keep(strip, strips)

    def flow_setup():
        kb[0] = one
        kb[nz + 1] = one

        def first(z, carry):
            temper, head, kind = wide(*oth, z), wide(*own, z), wide(soil, soil_rc, soil_c, z)
            look = looker(kind)
            liquid, alpha, poro, suction, satur = state(temper, head, look)
            cube = satur * satur * satur
            kb[z + 1] = look(3) * cube * jnp.exp(-2.0 * (1.0 - liquid))
            vb[z] = storage + poro * 0.9 * alpha * alpha * suction * cube
            xw[z] = head
            return carry

        levels(first, 0)

        def second(z, carry):
            above, ratio = carry
            hyd, cap, x = kb[z + 1], vb[z], xw[z]
            has = jnp.where(z < nz - 1, flow_vert * 0.5, 0.0)
            drain = jnp.where(z < nz - 1, 0.0, elevation)
            below = has * (hyd + kb[z + 2])
            side = flow_side * hyd
            inv = 1.0 / (cap + above + below + 4.0 * side - above * ratio)
            ratio = below * inv
            base = cap * x + elevation * (above - below) - drain * hyd
            bI[z] = jnp.where(free, base * inv, x)
            sI[z] = jnp.where(free, side * inv, 0.0)
            aI[z] = jnp.where(free, above * inv, 0.0)
            rI[z] = jnp.where(free, ratio, 0.0)
            return (below, ratio)

        zero = jnp.zeros((ROWS, COLS), jnp.float32)
        levels(second, (zero, zero))

    def flow_solve(dst, strip=None):
        for inner in range(INNER):
            last = inner == INNER - 1
            h, w = (nx, ny) if last else (ROWS, COLS)

            def forward(z, value):
                x = xw[z]
                near = pltpu.roll(x, 1, 0) + pltpu.roll(x, ROWS - 1, 0)
                near = near[:h, :w] + (pltpu.roll(x, 1, 1) + pltpu.roll(x, COLS - 1, 1))[:h, :w]
                value = bI[z, :h, :w] + sI[z, :h, :w] * near + aI[z, :h, :w] * value
                vb[z, :h, :w] = value
                return value

            zero = jnp.zeros((h, w), jnp.float32)
            levels(forward, zero)

            def backward(z, carry):
                lower, strips = carry
                solved = vb[z, :h, :w] + rI[z, :h, :w] * lower
                if last:
                    dst[z] = solved
                    if strip is not None:
                        strips = packed(z, solved, strips)
                else:
                    xw[z] = solved
                return (solved, strips)

            unused, strips = levels(backward, (zero, no_strips(zero.dtype)), down=False)
            if last and strip is not None:
                keep(strip, strips)

    @pl.when(is_heat)
    def _():
        heat_setup()
        heat_solve(res, it_cs)

    @pl.when(jnp.logical_not(is_heat))
    def _():
        flow_setup()
        flow_solve(res, it_cs)

    it_wait = edges(res, it_rc, it_cs, it_c, 2)
    it_wait()

    @pl.when(is_heat)
    def _():
        def fill(z, carry):
            xw[z] = wide(res, it_rc, it_c, z)
            return carry

        levels(fill, 0)
        heat_solve(res2)

    @pl.when(jnp.logical_not(is_heat))
    def _():
        def fill(z, carry):
            x = wide(res, it_rc, it_c, z)
            xw[z] = x
            bI[z] = jnp.where(free, bI[z], x)
            return carry

        levels(fill, 0)
        flow_solve(res2)

    lanes = pl.ds(pl.multiple_of(c * ny, ny), ny)
    moves = []
    for k in range(1, n_col):
        to = lax.rem(c + k, n_col)
        moves.append(
            remote(res2.at[pl.ds(to * zs, zs)], out.at[0, :, :, lanes], fin_s.at[k - 1], fin_r.at[k - 1], col=to)
        )
    local = pltpu.make_async_copy(res2.at[pl.ds(c * zs, zs)], out.at[0, :, :, lanes], loc_sem.at[1])
    for move in moves:
        move.start()
    local.start()
    local.wait()
    for move in moves:
        move.wait()


def solution(mesh):
    n_grp, n_col = mesh.shape["grp"], mesh.shape["col"]

    def on_device(fields, soil_type, surface, heat_cond, heat_capacity, porosity, sat_cond, vg_alpha):
        nz, nx, ny = soil_type.shape
        f32, i32 = jnp.float32, jnp.int32
        whole = lambda t: pltpu.VMEM((nz, nx, ny), t)
        tile = lambda t: pltpu.VMEM((nz, 8, ny), t)
        strip = lambda t: pltpu.VMEM((2, ROWS, ny), t)
        field = pltpu.VMEM((nz, ROWS, COLS), f32)
        dma = lambda *s: pltpu.SemaphoreType.DMA(s)
        part = pltpu.VMEM((2, nx, ny), f32)
        scratch = [
            whole(i32), pltpu.VMEM((nx, ny), f32), pltpu.SMEM((5, heat_cond.shape[0]), f32),
            whole(f32), whole(f32), tile(f32), tile(f32), part, strip(f32), strip(f32),
            tile(i32), pltpu.VMEM((2, nx, ny), i32), strip(i32),
            whole(f32), tile(f32), part, strip(f32), whole(f32),
            field, field, field, field, field, field, pltpu.VMEM((nz + 2, ROWS, COLS), f32),
            dma(9), dma(n_col - 1), dma(n_col - 1), dma(n_col + 2), dma(n_col + 2), dma(3, 8), dma(3, 8),
            dma(n_col - 1), dma(n_col - 1),
        ]
        anywhere = pl.BlockSpec(memory_space=pl.ANY)
        return pl.pallas_call(
            functools.partial(kernel, n_grp, n_col),
            out_shape=jax.ShapeDtypeStruct(fields.shape, f32),
            in_specs=[anywhere] * 8,
            out_specs=anywhere,
            scratch_shapes=scratch,
            compiler_params=pltpu.CompilerParams(
                collective_id=0, has_side_effects=True, vmem_limit_bytes=58 * 2**20
            ),
            name="step",
        )(fields, soil_type, surface, heat_cond, heat_capacity, porosity, sat_cond, vg_alpha)

    in_specs = (
        P("sec", "col", "grp", None), P(None, "grp", "col"), P("grp", "col"),
        P(), P(), P(), P(), P(),
    )
    return jax.shard_map(
        on_device, mesh=mesh, in_specs=in_specs, out_specs=P("sec", "col", "grp", None), check_vma=False
    )
```
